32 devices in a mesh: blk: 32 (over z, y, x, core).
Axes of the slice: x: 2, y: 2, z: 4, core: 2. Of those that a mesh axis runs over, the one named last changes fastest.
Arguments:
- embeddings: bfloat16 [65536, 1024], P('blk'), may hold values from -400 to 400
- centroid_codes: bfloat16 [16384, 1024], P('blk'), may hold values from -0.1875 to 0.1875
- centroid_scales: bfloat16 [16384], P('blk'), may hold values from 0.5 to 2
- log_normalizers: bfloat16 [65536], P('blk'), may hold values from 1 to 4
Outputs:
- new_centroids: float32 [16384, 1024], P('blk')
- mass_log: float32 [16384], P('blk')
- point_mass: float32 [65536], P('blk')
The draws below stay inside these ranges and needn't reach their ends.
All inputs are finite; a program needn't handle non-finite values.
Results may differ from the reference program's by a relative error of at most 0.004.
Values may be sent and summed in bfloat16 or wider, within the bound.
No kernel may reach another device: no remote copies, remote signals or barrier semaphores. Data moves between devices by JAX's collectives and lax.ppermute only.
A program may use at most 64 MiB of HBM per device.

```python
import math
import jax
import jax.numpy as jnp
from jax import lax

D = 1024
K_DEV = 512
P_DEV = 2048
STEPS = 2
CENTROIDS = 16384
POINTS = 65536
N_BLK = 32


def draw_embeddings(key, part):
    first, second, third = jax.random.split(key, 3)
    row_scale = jnp.exp(jax.random.uniform(second, (POINTS, 1), jnp.float32, 0.0, math.log(10.0)))
    col_scale = jnp.exp(jax.random.uniform(third, (1, D), jnp.float32, 0.0, math.log(10.0)))
    base = jnp.clip(jax.random.normal(first, (POINTS, D), jnp.float32), -4.0, 4.0)
    return (base * row_scale * col_scale).astype(jnp.bfloat16)


def block_levels(rng, extent, shards, low, high):
    def one(axis_at, shards_of):
        draws = jax.random.uniform(jax.random.fold_in(jax.random.fold_in(rng, 6), axis_at), (shards_of,), jnp.float32, low / len(shards), high / len(shards))
        return jnp.repeat(jnp.exp(draws), extent[axis_at] // shards_of).reshape((-1,) + (1,) * (len(extent) - axis_at - 1))

    gain = one(*shards[0])
    for cut in shards[1:]:
        gain = gain * one(*cut)
    return gain


def noise(rng, dims, scale, most, cuts=(), dtype=jnp.bfloat16):
    array = jax.random.normal(rng, dims, jnp.float32) * scale
    if len(cuts) > 0:
        array = block_levels(rng, dims, cuts, -0.22, 0.18) * array
    return jnp.clip(array, min=-most, max=most).astype(dtype)


def setup_inputs(seed: int = 0) -> dict:
    arg_keys = jax.random.split(jax.random.key(seed), 5)
    embeddings = draw_embeddings(jax.random.fold_in(arg_keys[4], 71), 0)
    centroid_codes = noise(arg_keys[1], (CENTROIDS, D), D ** -0.5, 0.1875, ((0, 32),))
    centroid_scales = jnp.clip(jnp.exp(math.log(2.0) - 1.3862944 * jax.random.uniform(arg_keys[2], (CENTROIDS,), jnp.float32) ** block_levels(arg_keys[2], (CENTROIDS,), ((0, 32),), -0.2, 0.2)), 0.5, 2.0).astype(jnp.bfloat16)
    log_normalizers = jnp.clip(1.0 + 3.0 * jax.random.uniform(arg_keys[3], (POINTS,), jnp.float32) ** block_levels(arg_keys[3], (POINTS,), ((0, 32),), -0.2, 0.2), 1.0, 4.0).astype(jnp.bfloat16)
    return {"embeddings": embeddings, "centroid_codes": centroid_codes, "centroid_scales": centroid_scales, "log_normalizers": log_normalizers}


def weigh(unit_rows, log_values, codes, scales):
    similarity = jnp.dot(unit_rows, codes.T, preferred_element_type=jnp.float32)
    weights = jnp.exp(similarity * scales.astype(jnp.float32)[None, :] - log_values.astype(jnp.float32)[:, None])
    weights_low = weights.astype(jnp.bfloat16)
    numerator = lax.dot_general(weights_low, unit_rows, (((0,), (0,)), ((), ())), preferred_element_type=jnp.float32)
    return (numerator, lax.optimization_barrier(jnp.sum(weights, axis=0)), lax.optimization_barrier(jnp.sum(weights, axis=1)))

def weigh_bundle(bundle):
    return weigh(bundle[0], bundle[1], bundle[2], bundle[3])

def reference(embeddings, centroid_codes, centroid_scales, log_normalizers):
    wide_points = embeddings.astype(jnp.float32)
    unit_rows = (wide_points * lax.rsqrt(lax.optimization_barrier(jnp.mean(wide_points * wide_points, axis=1, keepdims=True)) + 1e-06)).astype(jnp.bfloat16)
    unit_blocks = unit_rows.reshape(N_BLK, P_DEV, D)
    norm_blocks = log_normalizers.reshape(N_BLK, P_DEV)
    code_blocks = centroid_codes.reshape(N_BLK, K_DEV, D)
    scale_blocks = centroid_scales.reshape(N_BLK, K_DEV)
    numerator = jnp.zeros((N_BLK, K_DEV, D), jnp.float32)
    weight_sum = jnp.zeros((N_BLK, K_DEV), jnp.float32)
    point_total = jnp.zeros((N_BLK, P_DEV), jnp.float32)
    for offset in range(STEPS + 1):
        rolled_codes = jnp.roll(code_blocks, offset, axis=0)
        rolled_scales = jnp.roll(scale_blocks, offset, axis=0)
        part_numer, part_sum, part_total = lax.map(weigh_bundle, (unit_blocks, norm_blocks, rolled_codes, rolled_scales))
        numerator = numerator + jnp.roll(part_numer, -offset, axis=0)
        weight_sum = weight_sum + jnp.roll(part_sum, -offset, axis=0)
        point_total = point_total + part_total
    numerator = numerator.reshape(CENTROIDS, D)
    new_centroids = numerator * lax.rsqrt(lax.optimization_barrier(jnp.mean(numerator * numerator, axis=1, keepdims=True)) + 1e-06)
    return (new_centroids, jnp.log(weight_sum.reshape(CENTROIDS)), jnp.log(point_total.reshape(POINTS)))
```

```python
import jax
import jax.numpy as jnp
from jax import lax
from jax.sharding import PartitionSpec as P

PARTS = 2
EXTRA = 16


def shift(value, steps):
    count = lax.axis_size("blk")
    return lax.ppermute(value, "blk", [(i, (i + steps) % count) for i in range(count)])


def partner(value):
    count = lax.axis_size("blk")
    return lax.ppermute(value, "blk", [(i, i ^ 1) for i in range(count)])


def weigh(unit_rows, log_values, codes, scales):
    similarity = jnp.dot(unit_rows, codes.T, preferred_element_type=jnp.float32)
    weights = jnp.exp(similarity * scales[None, :] - log_values[:, None])
    numerator = lax.dot_general(
        weights.astype(jnp.bfloat16),
        unit_rows,
        (((0,), (0,)), ((), ())),
        preferred_element_type=jnp.float32,
    )
    return numerator, jnp.sum(weights, axis=0), jnp.sum(weights, axis=1)


def on_device(embeddings, centroid_codes, centroid_scales, log_normalizers):
    odd = lax.axis_index("blk") % 2 == 1
    rows, width = centroid_codes.shape
    part = rows // PARTS
    scale_rows = jnp.pad(centroid_scales[None, :], ((0, EXTRA - 1), (0, width - rows)))
    received = []
    for k in range(PARTS):
        block = centroid_codes[k * part : (k + 1) * part]
        if k == 0:
            block = jnp.concatenate([block, scale_rows], axis=0)
        received.append(shift(block, 2))
    wide = embeddings.astype(jnp.float32)
    unit_rows = (
        wide * lax.rsqrt(jnp.mean(wide * wide, axis=1, keepdims=True) + 1e-06)
    ).astype(jnp.bfloat16)
    logs = log_normalizers.astype(jnp.float32)
    other_rows = partner(unit_rows)
    other_logs = partner(log_normalizers).astype(jnp.float32)
    scales = centroid_scales.astype(jnp.float32)
    own_numer, own_sum, point_total = weigh(unit_rows, logs, centroid_codes, scales)
    moved_scales = received[0][part, :rows].astype(jnp.float32)
    other_total = 0.0
    own_numers, own_sums, sent = [], [], []
    for k in range(PARTS):
        cut = slice(k * part, (k + 1) * part)
        codes = received[k][:part]
        numer, total, points = weigh(unit_rows, logs, codes, moved_scales[cut])
        numer2, total2, points2 = weigh(
            other_rows,
            other_logs,
            jnp.where(odd, codes, centroid_codes[cut]),
            jnp.where(odd, moved_scales[cut], scales[cut]),
        )
        point_total = point_total + points
        other_total = other_total + points2
        numer = numer + jnp.where(odd, numer2, 0.0)
        total = total + jnp.where(odd, total2, 0.0)
        own_numers.append(own_numer[cut] + jnp.where(odd, 0.0, numer2))
        own_sums.append(own_sum[cut] + jnp.where(odd, 0.0, total2))
        high = total.astype(jnp.bfloat16)
        low = (total - high.astype(jnp.float32)).astype(jnp.bfloat16)
        ends = jnp.pad(jnp.stack([high, low]), ((0, EXTRA - 2), (0, width - part)))
        sent.append(shift(jnp.concatenate([numer.astype(jnp.bfloat16), ends], axis=0), -2))
    point_total = point_total + partner(other_total)
    outs, sums = [], []
    for k in range(PARTS):
        back = sent[k].astype(jnp.float32)
        numer = own_numers[k] + back[:part]
        outs.append(numer * lax.rsqrt(jnp.mean(numer * numer, axis=1, keepdims=True) + 1e-06))
        sums.append(own_sums[k] + (back[part, :part] + back[part + 1, :part]))
    return (
        jnp.concatenate(outs, axis=0),
        jnp.log(jnp.concatenate(sums)),
        jnp.log(point_total),
    )


def solution(mesh):
    return jax.shard_map(
        on_device,
        mesh=mesh,
        in_specs=(P("blk", None), P("blk", None), P("blk"), P("blk")),
        out_specs=(P("blk", None), P("blk"), P("blk")),
        check_vma=False,
    )
```

```python
import functools

import jax
import jax.numpy as jnp
from jax import lax
from jax.experimental import pallas as pl
from jax.experimental.pallas import tpu as pltpu
from jax.sharding import PartitionSpec as P

PARTS = 2
EXTRA = 16
TILE = 512
LANES = 128
NORM = 256
F32 = jnp.float32
BF16 = jnp.bfloat16
VMEM = pl.BlockSpec(memory_space=pltpu.VMEM)
HBM = pl.BlockSpec(memory_space=pltpu.HBM)
SMEM = pl.BlockSpec(memory_space=pltpu.SMEM)


def shift(value, steps):
    count = lax.axis_size("blk")
    return lax.ppermute(value, "blk", [(i, (i + steps) % count) for i in range(count)])


def partner(value):
    count = lax.axis_size("blk")
    return lax.ppermute(value, "blk", [(i, i ^ 1) for i in range(count)])


def call(kernel, outs, scratch=(), specs=(), name=None, aliases=None, mib=12):
    return pl.pallas_call(
        kernel,
        out_shape=[jax.ShapeDtypeStruct(s, d) for s, d in outs],
        in_specs=list(specs),
        out_specs=[VMEM] * len(outs),
        scratch_shapes=list(scratch),
        input_output_aliases=aliases or {},
        compiler_params=pltpu.CompilerParams(vmem_limit_bytes=mib << 20),
        cost_estimate=pl.CostEstimate(flops=1000, bytes_accessed=1000, transcendentals=0),
        name=name,
    )


def column(row, rows):
    return jnp.transpose(jnp.broadcast_to(row, (LANES, rows)))


def weigh(codes, scale, points, logs, cut, weights, total):
    similarity = lax.dot_general(
        codes, points, (((1,), (1,)), ((), ())), preferred_element_type=F32
    )
    weight = jnp.exp(similarity * jnp.tile(scale, (1, TILE // LANES)) - logs[:, cut])
    weights[:, cut] = weight.astype(BF16)
    for lane in range(0, TILE, LANES):
        piece = weight[:, lane : lane + LANES]
        total = piece if total is None else total + piece
    return jnp.sum(weight, axis=0, keepdims=True), total


def row_of(total):
    return jnp.sum(jnp.transpose(total), axis=0, keepdims=True)


def tiles_of(count):
    return [slice(t * TILE, (t + 1) * TILE) for t in range(count // TILE)]


def norm_tile(raw, unit, cut):
    for start in range(cut.start, cut.stop, NORM):
        some = slice(start, start + NORM)
        wide = raw[some, :].astype(F32)
        scale = lax.rsqrt(jnp.mean(wide * wide, axis=1, keepdims=True) + 1e-06)
        unit[some, :] = (wide * scale).astype(BF16)


def block(part, codes, scales, fetch, unit, logs, weights, numer, sums, point_sum, add):
    cuts = [slice(k * part, (k + 1) * part) for k in range(codes.shape[0] // part)]
    wide = [column(scales[:, cut], part) for cut in cuts]
    totals = [None] * len(cuts)
    tiles = tiles_of(unit.shape[0])
    fetch(0)
    for t, tile in enumerate(tiles):
        points = unit[tile, :]
        if t + 1 < len(tiles):
            fetch(t + 1)
        line = 0.0
        for k, cut in enumerate(cuts):
            some, totals[k] = weigh(
                codes[cut, :], wide[k], points, logs, tile, weights.at[k], totals[k]
            )
            line = line + some
        point_sum[:, tile] = line
    for k, cut in enumerate(cuts):
        value = jnp.dot(weights[k], unit[...], preferred_element_type=F32)
        if add:
            numer[cut, :] += value
            sums[:, cut] += row_of(totals[k])
        else:
            numer[cut, :] = value
            sums[:, cut] = row_of(totals[k])


def local_kernel(
    part, odd, own_raw, other_raw, own_codes, scales, logs, other_logs,
    unit, other_unit, numer, sums, point_sum, other_sum,
    raw, codes, weights, sems, code_sem,
):
    tiles = tiles_of(unit.shape[0])

    def copies(source, at):
        return [
            pltpu.make_async_copy(source.at[tile, :], raw.at[at, tile, :], sems.at[at, t])
            for t, tile in enumerate(tiles)
        ]

    first, second = copies(own_raw, 0), copies(other_raw, 1)
    code_copy = pltpu.make_async_copy(own_codes, codes, code_sem)
    for copy in [first[0], code_copy] + first[1:] + second:
        copy.start()

    def fetch(t):
        first[t].wait()
        norm_tile(raw.at[0], unit, tiles[t])
        if t == 0:
            code_copy.wait()

    def fetch_other(t):
        second[t].wait()
        norm_tile(raw.at[1], other_unit, tiles[t])

    block(part, codes, scales, fetch, unit, logs, weights, numer, sums, point_sum, False)

    @pl.when(odd[0] == 0)
    def _():
        block(
            part, codes, scales, fetch_other, other_unit, other_logs, weights, numer, sums, other_sum, True
        )

    @pl.when(odd[0] == 1)
    def _():
        for t in range(len(tiles)):
            fetch_other(t)
        other_sum[...] = jnp.zeros_like(other_sum)


def moved_kernel(
    k, part, odd, codes, scales, points, logs, others, other_logs, sums0, point_before, other_before,
    sent, sums, point_sum, other_sum, weights, numer,
):
    rows = PARTS * part
    cut = slice(k * part, (k + 1) * part)
    scale = column(scales[part : part + EXTRA, :rows].astype(F32)[:1, cut], part)

    def weigh_all(rows, row_logs, before, after):
        total = None
        for tile in tiles_of(rows.shape[0]):
            line, total = weigh(
                codes[:part, :], scale, rows[tile, :], row_logs, tile, weights, total
            )
            after[:, tile] = before[:, tile] + line
        return row_of(total)

    sums[...] = sums0[...]
    sums[:, cut] = weigh_all(points, logs, point_before, point_sum)

    @pl.when(odd[0] == 0)
    def _():
        other_sum[...] = other_before[...]
        value = jnp.dot(weights[...], points[...], preferred_element_type=F32)
        sent[:part, :] = value.astype(BF16)

    @pl.when(odd[0] == 1)
    def _():
        numer[...] = jnp.dot(weights[...], points[...], preferred_element_type=F32)
        sums[:, cut] += weigh_all(others, other_logs, other_before, other_sum)
        value = numer[...] + jnp.dot(weights[...], others[...], preferred_element_type=F32)
        sent[:part, :] = value.astype(BF16)

    if sent.shape[0] > part:
        high = sums[...].astype(BF16).astype(F32)
        row = lax.broadcasted_iota(jnp.int32, (EXTRA, rows), 0)
        ends = jnp.where(row == 0, high, jnp.where(row == 1, sums[...] - high, 0.0))
        sent[part:, :] = jnp.zeros((EXTRA, sent.shape[1]), BF16)
        sent[part:, :rows] = ends.astype(BF16)


def last_kernel(k, part, numer, back, sums, *refs):
    *refs, out, mass = refs if back.shape[0] > part else (*refs, None)
    rows = out.shape[0]
    start = pl.multiple_of(pl.program_id(0) * rows, rows)
    total = numer[pl.ds(k * part + start, rows), :] + back[pl.ds(start, rows), :].astype(F32)
    out[...] = total * lax.rsqrt(jnp.mean(total * total, axis=1, keepdims=True) + 1e-06)
    if mass is not None:
        ends = back[part:, : mass.shape[1]].astype(F32)
        mass[...] = jnp.log(sums[...] + jnp.sum(ends, axis=0, keepdims=True))


def last(k, part, numer, back, sums, before):
    width = back.shape[1]
    steps = 2
    more = [] if before is None else [before]
    outs = [numer, sums] if back.shape[0] > part else [numer]
    return pl.pallas_call(
        functools.partial(last_kernel, k, part),
        grid=(steps,),
        out_shape=[jax.ShapeDtypeStruct(out.shape, F32) for out in outs],
        in_specs=[VMEM, VMEM, VMEM] + [HBM] * len(more),
        out_specs=[pl.BlockSpec((part // steps, width), lambda i: (k * steps + i, 0)), VMEM][: len(outs)],
        input_output_aliases={3: 0} if more else {},
        compiler_params=pltpu.CompilerParams(vmem_limit_bytes=6 << 20),
        cost_estimate=pl.CostEstimate(flops=1000, bytes_accessed=1000, transcendentals=0),
        name=f"last{k}",
    )(numer, back, sums, *more)


def on_device(embeddings, centroid_codes, centroid_scales, log_normalizers):
    odd = (lax.axis_index("blk") & 1).astype(jnp.int32).reshape(1)
    rows, width = centroid_codes.shape
    points = embeddings.shape[0]
    part = rows // PARTS
    cuts = [slice(k * part, (k + 1) * part) for k in range(PARTS)]
    scale_rows = jnp.pad(centroid_scales.reshape(1, rows), ((0, EXTRA - 1), (0, width - rows)))
    received = [shift(jnp.concatenate([centroid_codes[cuts[0]], scale_rows], axis=0), 2)]
    received += [shift(lax.optimization_barrier(centroid_codes)[cut], 2) for cut in cuts[1:]]
    scales = centroid_scales.astype(F32).reshape(1, rows)
    logs = log_normalizers.astype(F32).reshape(1, points)
    other_raw = partner(embeddings)
    other_logs = partner(log_normalizers).astype(F32).reshape(1, points)
    line = ((1, points), F32)
    units = ((points, width), BF16)
    unit_rows, other_rows, numer, own_sum, point_total, other_total = call(
        functools.partial(local_kernel, part),
        [units, units, ((rows, width), F32), ((1, rows), F32), line, line],
        [
            pltpu.VMEM((2, points, width), BF16),
            pltpu.VMEM((rows, width), BF16),
            pltpu.VMEM((PARTS, part, points), BF16),
            pltpu.SemaphoreType.DMA((2, points // TILE)),
            pltpu.SemaphoreType.DMA(()),
        ],
        [SMEM, HBM, HBM, HBM] + [VMEM] * 3,
        "local",
        mib=24,
    )(odd, embeddings, other_raw, centroid_codes, scales, logs, other_logs)
    back = []
    sums = jnp.zeros((1, rows), F32)
    for k in range(PARTS):
        more = EXTRA if k == PARTS - 1 else 0
        sent, sums, point_total, other_total = call(
            functools.partial(moved_kernel, k, part),
            [((part + more, width), BF16), ((1, rows), F32), line, line],
            [pltpu.VMEM((part, points), BF16), pltpu.VMEM((part, width), F32)],
            [SMEM] + [VMEM] * 9,
            f"moved{k}",
        )(
            odd, received[k], received[0], unit_rows, logs, other_rows, other_logs, sums,
            point_total, other_total,
        )
        back.append(shift(sent, -2))
    back[0], other_total = lax.optimization_barrier((back[0], other_total))
    point_mass = jnp.log(point_total + partner(other_total))
    back[-1], point_mass = lax.optimization_barrier((back[-1], point_mass))
    new_centroids = None
    for k in range(PARTS):
        new_centroids, *mass_log = last(k, part, numer, back[k], own_sum, new_centroids)
    return (new_centroids, mass_log[0].reshape(rows), point_mass.reshape(points))


def solution(mesh):
    return jax.shard_map(
        on_device,
        mesh=mesh,
        in_specs=(P("blk", None), P("blk", None), P("blk"), P("blk")),
        out_specs=(P("blk", None), P("blk"), P("blk")),
        check_vma=False,
    )
```

```python
import functools

import jax
import jax.numpy as jnp
from jax import lax
from jax.experimental import pallas as pl
from jax.experimental.pallas import tpu as pltpu
from jax.sharding import PartitionSpec as P

HALVES = 2
SIZES = (256, 256)
EXTRA = 16
TILE = 512
LANES = 128
NORM = 256
F32 = jnp.float32
BF16 = jnp.bfloat16
VMEM = pl.BlockSpec(memory_space=pltpu.VMEM)
HBM = pl.BlockSpec(memory_space=pltpu.HBM)
SMEM = pl.BlockSpec(memory_space=pltpu.SMEM)


def shift(value, steps):
    count = lax.axis_size("blk")
    return lax.ppermute(value, "blk", [(i, (i + steps) % count) for i in range(count)])


def partner(value):
    count = lax.axis_size("blk")
    return lax.ppermute(value, "blk", [(i, i ^ 1) for i in range(count)])


def call(kernel, outs, scratch=(), specs=(), name=None, aliases=None, mib=12):
    return pl.pallas_call(
        kernel,
        out_shape=[jax.ShapeDtypeStruct(s, d) for s, d in outs],
        in_specs=list(specs),
        out_specs=[VMEM] * len(outs),
        scratch_shapes=list(scratch),
        input_output_aliases=aliases or {},
        compiler_params=pltpu.CompilerParams(vmem_limit_bytes=mib << 20),
        cost_estimate=pl.CostEstimate(flops=1000, bytes_accessed=1000, transcendentals=0),
        name=name,
    )


def column(row, rows):
    return jnp.transpose(jnp.broadcast_to(row, (LANES, rows)))


def weigh(codes, scale, points, logs, cut, weights, total):
    similarity = lax.dot_general(
        codes, points, (((1,), (1,)), ((), ())), preferred_element_type=F32
    )
    weight = jnp.exp(similarity * jnp.tile(scale, (1, TILE // LANES)) - logs[:, cut])
    weights[:, cut] = weight.astype(BF16)
    for lane in range(0, TILE, LANES):
        piece = weight[:, lane : lane + LANES]
        total = piece if total is None else total + piece
    return jnp.sum(weight, axis=0, keepdims=True), total


def row_of(total):
    return jnp.sum(jnp.transpose(total), axis=0, keepdims=True)


def tiles_of(count):
    return [slice(t * TILE, (t + 1) * TILE) for t in range(count // TILE)]


def norm_tile(raw, unit, cut):
    for start in range(cut.start, cut.stop, NORM):
        some = slice(start, start + NORM)
        wide = raw[some, :].astype(F32)
        scale = lax.rsqrt(jnp.mean(wide * wide, axis=1, keepdims=True) + 1e-06)
        unit[some, :] = (wide * scale).astype(BF16)


def block(part, codes, scales, fetch, unit, logs, weights, numer, sums, point_sum, add):
    cuts = [slice(k * part, (k + 1) * part) for k in range(codes.shape[0] // part)]
    wide = [column(scales[:, cut], part) for cut in cuts]
    totals = [None] * len(cuts)
    tiles = tiles_of(unit.shape[0])
    fetch(0)
    for t, tile in enumerate(tiles):
        points = unit[tile, :]
        if t + 1 < len(tiles):
            fetch(t + 1)
        line = 0.0
        for k, cut in enumerate(cuts):
            some, totals[k] = weigh(
                codes[cut, :], wide[k], points, logs, tile, weights.at[k], totals[k]
            )
            line = line + some
        point_sum[:, tile] = line
    for k, cut in enumerate(cuts):
        value = jnp.dot(weights[k], unit[...], preferred_element_type=F32)
        if add:
            numer[cut, :] += value
            sums[:, cut] += row_of(totals[k])
        else:
            numer[cut, :] = value
            sums[:, cut] = row_of(totals[k])


def local_kernel(
    part, odd, own_raw, other_raw, own_codes, scales, logs, other_logs,
    unit, other_unit, numer, sums, point_sum, other_sum,
    raw, codes, weights, sems, code_sem,
):
    tiles = tiles_of(unit.shape[0])

    def copies(source, at):
        return [
            pltpu.make_async_copy(source.at[tile, :], raw.at[at, tile, :], sems.at[at, t])
            for t, tile in enumerate(tiles)
        ]

    first, second = copies(own_raw, 0), copies(other_raw, 1)
    code_copy = pltpu.make_async_copy(own_codes, codes, code_sem)
    for copy in [first[0], code_copy] + first[1:] + second:
        copy.start()

    def fetch(t):
        first[t].wait()
        norm_tile(raw.at[0], unit, tiles[t])
        if t == 0:
            code_copy.wait()

    def fetch_other(t):
        second[t].wait()
        norm_tile(raw.at[1], other_unit, tiles[t])

    block(part, codes, scales, fetch, unit, logs, weights, numer, sums, point_sum, False)

    @pl.when(odd[0] == 0)
    def _():
        block(
            part, codes, scales, fetch_other, other_unit, other_logs, weights, numer, sums, other_sum, True
        )

    @pl.when(odd[0] == 1)
    def _():
        for t in range(len(tiles)):
            fetch_other(t)
        other_sum[...] = jnp.zeros_like(other_sum)


def moved_kernel(
    cut, odd, codes, scales, points, logs, others, other_logs, sums0, point_before, other_before,
    sent, sums, point_sum, other_sum, weights, numer,
):
    part, rows = cut.stop - cut.start, sums0.shape[1]
    first = scales.shape[0] - EXTRA
    scale = column(scales[first:, :rows].astype(F32)[:1, cut], part)

    def weigh_all(rows, row_logs, before, after):
        total = None
        for tile in tiles_of(rows.shape[0]):
            line, total = weigh(
                codes[:part, :], scale, rows[tile, :], row_logs, tile, weights, total
            )
            after[:, tile] = before[:, tile] + line
        return row_of(total)

    sums[...] = sums0[...]
    sums[:, cut] = weigh_all(points, logs, point_before, point_sum)

    @pl.when(odd[0] == 0)
    def _():
        other_sum[...] = other_before[...]
        value = jnp.dot(weights[...], points[...], preferred_element_type=F32)
        sent[:part, :] = value.astype(BF16)

    @pl.when(odd[0] == 1)
    def _():
        numer[...] = jnp.dot(weights[...], points[...], preferred_element_type=F32)
        sums[:, cut] += weigh_all(others, other_logs, other_before, other_sum)
        value = numer[...] + jnp.dot(weights[...], others[...], preferred_element_type=F32)
        sent[:part, :] = value.astype(BF16)


def first_rows(cut, numer, back, out):
    rows = out.shape[0]
    start = pl.multiple_of(pl.program_id(0) * rows, rows)
    total = numer[pl.ds(cut.start + start, rows), :] + back[pl.ds(start, rows), :].astype(F32)
    out[...] = total * lax.rsqrt(jnp.mean(total * total, axis=1, keepdims=True) + 1e-06)


def last_rows(cut, numer, back, sums, back_sums, before, out, mass):
    del before
    first_rows(cut, numer, back, out)
    mass[...] = jnp.log(sums[...] + back_sums[...])


def finish(cut, numer, back, *more):
    part, width = back.shape
    steps = 2
    block = part // steps
    shapes = [jax.ShapeDtypeStruct(numer.shape, F32)]
    specs = [pl.BlockSpec((block, width), lambda i: (cut.start // block + i, 0))]
    if more:
        shapes.append(jax.ShapeDtypeStruct(more[0].shape, F32))
        specs.append(VMEM)
    return pl.pallas_call(
        functools.partial(last_rows if more else first_rows, cut),
        grid=(steps,),
        out_shape=shapes,
        in_specs=[VMEM, VMEM] + ([VMEM, VMEM, HBM] if more else []),
        out_specs=specs,
        input_output_aliases={4: 0} if more else {},
        compiler_params=pltpu.CompilerParams(vmem_limit_bytes=6 << 20),
        cost_estimate=pl.CostEstimate(flops=1000, bytes_accessed=1000, transcendentals=0),
        name=f"finish{cut.start}",
    )(numer, back, *more)


def on_device(embeddings, centroid_codes, centroid_scales, log_normalizers):
    odd = (lax.axis_index("blk") & 1).astype(jnp.int32).reshape(1)
    rows, width = centroid_codes.shape
    points = embeddings.shape[0]
    half = rows // HALVES
    ends = [sum(SIZES[: k + 1]) for k in range(len(SIZES))]
    cuts = [slice(end - size, end) for end, size in zip(ends, SIZES)]
    assert ends[-1] == rows
    row = lax.broadcasted_iota(jnp.int32, (cuts[0].stop + EXTRA, rows), 0)
    first = centroid_codes[: cuts[0].stop + EXTRA]
    first = jnp.concatenate(
        [jnp.where(row < cuts[0].stop, first[:, :rows], centroid_scales), first[:, rows:]], axis=1
    )
    received = [shift(first, 2)]
    received += [shift(lax.optimization_barrier(centroid_codes)[cut], 2) for cut in cuts[1:]]
    scales = centroid_scales.astype(F32).reshape(1, rows)
    logs = log_normalizers.astype(F32).reshape(1, points)
    other_raw = partner(embeddings)
    other_logs = partner(log_normalizers).astype(F32).reshape(1, points)
    line = ((1, points), F32)
    units = ((points, width), BF16)
    unit_rows, other_rows, numer, own_sum, point_total, other_total = call(
        functools.partial(local_kernel, half),
        [units, units, ((rows, width), F32), ((1, rows), F32), line, line],
        [
            pltpu.VMEM((2, points, width), BF16),
            pltpu.VMEM((rows, width), BF16),
            pltpu.VMEM((HALVES, half, points), BF16),
            pltpu.SemaphoreType.DMA((2, points // TILE)),
            pltpu.SemaphoreType.DMA(()),
        ],
        [SMEM, HBM, HBM, HBM] + [VMEM] * 3,
        "local",
        mib=24,
    )(odd, embeddings, other_raw, centroid_codes, scales, logs, other_logs)
    back = []
    sums = jnp.zeros((1, rows), F32)
    for k, cut in enumerate(cuts):
        part = cut.stop - cut.start
        sent, sums, point_total, other_total = call(
            functools.partial(moved_kernel, cut),
            [((part, width), BF16), ((1, rows), F32), line, line],
            [pltpu.VMEM((part, points), BF16), pltpu.VMEM((part, width), F32)],
            [SMEM] + [VMEM] * 9,
            f"moved{k}",
        )(
            odd, received[k], received[0], unit_rows, logs, other_rows, other_logs, sums,
            point_total, other_total,
        )
        back.append(shift(sent, -2))
    *back[:-1], other_total, sums = lax.optimization_barrier((*back[:-1], other_total, sums))
    point_mass = jnp.log(point_total + partner(other_total))
    back_sums = shift(sums, -2)
    (new_centroids,) = finish(cuts[0], numer, back[0])
    back[1], point_mass = lax.optimization_barrier((back[1], point_mass))
    new_centroids, mass_log = finish(cuts[1], numer, back[1], own_sum, back_sums, new_centroids)
    return (new_centroids, mass_log.reshape(rows), point_mass.reshape(points))


def solution(mesh):
    return jax.shard_map(
        on_device,
        mesh=mesh,
        in_specs=(P("blk", None), P("blk", None), P("blk"), P("blk")),
        out_specs=(P("blk", None), P("blk"), P("blk")),
        check_vma=False,
    )
```

```python
import functools

import jax
import jax.numpy as jnp
from jax import lax
from jax.experimental import pallas as pl
from jax.experimental.pallas import tpu as pltpu
from jax.sharding import PartitionSpec as P

HALVES = 2
SIZES = (256, 256)
EXTRA = 16
TILE = 512
LANES = 128
NORM = 256
F32 = jnp.float32
BF16 = jnp.bfloat16
VMEM = pl.BlockSpec(memory_space=pltpu.VMEM)
HBM = pl.BlockSpec(memory_space=pltpu.HBM)
SMEM = pl.BlockSpec(memory_space=pltpu.SMEM)


def shift(value, steps):
    count = lax.axis_size("blk")
    return lax.ppermute(value, "blk", [(i, (i + steps) % count) for i in range(count)])


def partner(value):
    count = lax.axis_size("blk")
    return lax.ppermute(value, "blk", [(i, i ^ 1) for i in range(count)])


def call(kernel, outs, scratch=(), specs=(), name=None, aliases=None, mib=12):
    return pl.pallas_call(
        kernel,
        out_shape=[jax.ShapeDtypeStruct(s, d) for s, d in outs],
        in_specs=list(specs),
        out_specs=[VMEM] * len(outs),
        scratch_shapes=list(scratch),
        input_output_aliases=aliases or {},
        compiler_params=pltpu.CompilerParams(vmem_limit_bytes=mib << 20),
        cost_estimate=pl.CostEstimate(flops=1000, bytes_accessed=1000, transcendentals=0),
        name=name,
    )


def column(row, rows):
    return jnp.transpose(jnp.broadcast_to(row, (LANES, rows)))


def weigh(codes, scale, points, logs, cut, weights, total):
    similarity = lax.dot_general(
        codes, points, (((1,), (1,)), ((), ())), preferred_element_type=F32
    )
    weight = jnp.exp(similarity * jnp.tile(scale, (1, TILE // LANES)) - logs[:, cut])
    weights[:, cut] = weight.astype(BF16)
    for lane in range(0, TILE, LANES):
        piece = weight[:, lane : lane + LANES]
        total = piece if total is None else total + piece
    return jnp.sum(weight, axis=0, keepdims=True), total


def row_of(total):
    return jnp.sum(jnp.transpose(total), axis=0, keepdims=True)


def tiles_of(count):
    return [slice(t * TILE, (t + 1) * TILE) for t in range(count // TILE)]


def norm_tile(raw, unit, cut):
    for start in range(cut.start, cut.stop, NORM):
        some = slice(start, start + NORM)
        wide = raw[some, :].astype(F32)
        scale = lax.rsqrt(jnp.mean(wide * wide, axis=1, keepdims=True) + 1e-06)
        unit[some, :] = (wide * scale).astype(BF16)


def block(part, codes, scales, fetch, unit, logs, weights, numer, sums, point_sum, add):
    cuts = [slice(k * part, (k + 1) * part) for k in range(codes.shape[0] // part)]
    wide = [column(scales[:, cut], part) for cut in cuts]
    totals = [None] * len(cuts)
    tiles = tiles_of(unit.shape[0])
    fetch(0)
    for t, tile in enumerate(tiles):
        points = unit[tile, :]
        if t + 1 < len(tiles):
            fetch(t + 1)
        line = 0.0
        for k, cut in enumerate(cuts):
            some, totals[k] = weigh(
                codes[cut, :], wide[k], points, logs, tile, weights.at[k], totals[k]
            )
            line = line + some
        point_sum[:, tile] = line
    for k, cut in enumerate(cuts):
        value = jnp.dot(weights[k], unit[...], preferred_element_type=F32)
        if add:
            numer[cut, :] += value
            sums[:, cut] += row_of(totals[k])
        else:
            numer[cut, :] = value
            sums[:, cut] = row_of(totals[k])


def local_kernel(
    part, odd, own_raw, other_raw, own_codes, scales, logs, other_logs,
    unit, other_unit, numer, sums, point_sum, other_sum,
    raw, codes, weights, sems, code_sem,
):
    tiles = tiles_of(unit.shape[0])

    def copies(source, at):
        return [
            pltpu.make_async_copy(source.at[tile, :], raw.at[at, tile, :], sems.at[at, t])
            for t, tile in enumerate(tiles)
        ]

    first, second = copies(own_raw, 0), copies(other_raw, 1)
    code_copy = pltpu.make_async_copy(own_codes, codes, code_sem)
    for copy in [first[0], code_copy] + first[1:] + second:
        copy.start()

    def fetch(t):
        first[t].wait()
        norm_tile(raw.at[0], unit, tiles[t])
        if t == 0:
            code_copy.wait()

    def fetch_other(t):
        second[t].wait()
        norm_tile(raw.at[1], other_unit, tiles[t])

    block(part, codes, scales, fetch, unit, logs, weights, numer, sums, point_sum, False)

    @pl.when(odd[0] == 0)
    def _():
        block(
            part, codes, scales, fetch_other, other_unit, other_logs, weights, numer, sums, other_sum, True
        )

    @pl.when(odd[0] == 1)
    def _():
        for t in range(len(tiles)):
            fetch_other(t)
        other_sum[...] = jnp.zeros_like(other_sum)


def moved_kernel(
    cut, odd, codes, scales, points, logs, others, other_logs, sums0, point_before, other_before,
    sent, sums, point_sum, other_sum, weights, numer,
):
    part, rows = cut.stop - cut.start, sums0.shape[1]
    first = scales.shape[0] - EXTRA
    scale = column(scales[first:, :rows].astype(F32)[:1, cut], part)

    def weigh_all(rows, row_logs, before, after):
        total = None
        for tile in tiles_of(rows.shape[0]):
            line, total = weigh(
                codes[:part, :], scale, rows[tile, :], row_logs, tile, weights, total
            )
            after[:, tile] = before[:, tile] + line
        return row_of(total)

    sums[...] = sums0[...]
    sums[:, cut] = weigh_all(points, logs, point_before, point_sum)

    @pl.when(odd[0] == 0)
    def _():
        other_sum[...] = other_before[...]
        value = jnp.dot(weights[...], points[...], preferred_element_type=F32)
        sent[:part, :] = value.astype(BF16)

    @pl.when(odd[0] == 1)
    def _():
        numer[...] = jnp.dot(weights[...], points[...], preferred_element_type=F32)
        sums[:, cut] += weigh_all(others, other_logs, other_before, other_sum)
        value = numer[...] + jnp.dot(weights[...], others[...], preferred_element_type=F32)
        sent[:part, :] = value.astype(BF16)


def first_rows(cut, numer, back, out):
    rows = out.shape[0]
    start = pl.multiple_of(pl.program_id(0) * rows, rows)
    total = numer[pl.ds(cut.start + start, rows), :] + back[pl.ds(start, rows), :].astype(F32)
    out[...] = total * lax.rsqrt(jnp.mean(total * total, axis=1, keepdims=True) + 1e-06)


def last_rows(cut, numer, back, sums, back_sums, before, out, mass):
    del before
    first_rows(cut, numer, back, out)
    mass[...] = jnp.log(sums[...] + back_sums[...])


def finish(cut, numer, back, *more):
    part, width = back.shape
    steps = 2
    block = part // steps
    shapes = [jax.ShapeDtypeStruct(numer.shape, F32)]
    specs = [pl.BlockSpec((block, width), lambda i: (cut.start // block + i, 0))]
    if more:
        shapes.append(jax.ShapeDtypeStruct(more[0].shape, F32))
        specs.append(VMEM)
    return pl.pallas_call(
        functools.partial(last_rows if more else first_rows, cut),
        grid=(steps,),
        out_shape=shapes,
        in_specs=[VMEM, VMEM] + ([VMEM, VMEM, HBM] if more else []),
        out_specs=specs,
        input_output_aliases={4: 0} if more else {},
        compiler_params=pltpu.CompilerParams(vmem_limit_bytes=6 << 20),
        cost_estimate=pl.CostEstimate(flops=1000, bytes_accessed=1000, transcendentals=0),
        name=f"finish{cut.start}",
    )(numer, back, *more)


def on_device(embeddings, centroid_codes, centroid_scales, log_normalizers):
    odd = (lax.axis_index("blk") & 1).astype(jnp.int32).reshape(1)
    rows, width = centroid_codes.shape
    points = embeddings.shape[0]
    half = rows // HALVES
    ends = [sum(SIZES[: k + 1]) for k in range(len(SIZES))]
    cuts = [slice(end - size, end) for end, size in zip(ends, SIZES)]
    assert ends[-1] == rows
    row = lax.broadcasted_iota(jnp.int32, (cuts[0].stop + EXTRA, rows), 0)
    first = centroid_codes[: cuts[0].stop + EXTRA]
    first = jnp.concatenate(
        [jnp.where(row < cuts[0].stop, first[:, :rows], centroid_scales), first[:, rows:]], axis=1
    )
    first, embeddings = lax.optimization_barrier((first, embeddings))
    received = [shift(first, 2)]
    received += [shift(lax.optimization_barrier(centroid_codes)[cut], 2) for cut in cuts[1:]]
    scales = centroid_scales.astype(F32).reshape(1, rows)
    logs = log_normalizers.astype(F32).reshape(1, points)
    other_raw = partner(embeddings)
    other_logs = partner(log_normalizers).astype(F32).reshape(1, points)
    line = ((1, points), F32)
    units = ((points, width), BF16)
    unit_rows, other_rows, numer, own_sum, point_total, other_total = call(
        functools.partial(local_kernel, half),
        [units, units, ((rows, width), F32), ((1, rows), F32), line, line],
        [
            pltpu.VMEM((2, points, width), BF16),
            pltpu.VMEM((rows, width), BF16),
            pltpu.VMEM((HALVES, half, points), BF16),
            pltpu.SemaphoreType.DMA((2, points // TILE)),
            pltpu.SemaphoreType.DMA(()),
        ],
        [SMEM, HBM, HBM, HBM] + [VMEM] * 3,
        "local",
        mib=40,
    )(odd, embeddings, other_raw, centroid_codes, scales, logs, other_logs)
    back = []
    sums = jnp.zeros((1, rows), F32)
    for k, cut in enumerate(cuts):
        part = cut.stop - cut.start
        sent, sums, point_total, other_total = call(
            functools.partial(moved_kernel, cut),
            [((part, width), BF16), ((1, rows), F32), line, line],
            [pltpu.VMEM((part, points), BF16), pltpu.VMEM((part, width), F32)],
            [SMEM] + [VMEM] * 9,
            f"moved{k}",
        )(
            odd, received[k], received[0], unit_rows, logs, other_rows, other_logs, sums,
            point_total, other_total,
        )
        back.append(shift(sent, -2))
    *back[:-1], other_total, sums = lax.optimization_barrier((*back[:-1], other_total, sums))
    point_mass = jnp.log(point_total + partner(other_total))
    back_sums = shift(sums, -2)
    (new_centroids,) = finish(cuts[0], numer, back[0])
    back[1], point_mass = lax.optimization_barrier((back[1], point_mass))
    new_centroids, mass_log = finish(cuts[1], numer, back[1], own_sum, back_sums, new_centroids)
    return (new_centroids, mass_log.reshape(rows), point_mass.reshape(points))


def solution(mesh):
    return jax.shard_map(
        on_device,
        mesh=mesh,
        in_specs=(P("blk", None), P("blk", None), P("blk"), P("blk")),
        out_specs=(P("blk", None), P("blk"), P("blk")),
        check_vma=False,
    )
```

```python
import functools

import jax
import jax.numpy as jnp
from jax import lax
from jax.experimental import pallas as pl
from jax.experimental.pallas import tpu as pltpu
from jax.sharding import PartitionSpec as P

HALVES = 2
SIZES = (256, 256)
EXTRA = 16
TILE = 1024
LANES = 128
NORM = 256
F32 = jnp.float32
BF16 = jnp.bfloat16
VMEM = pl.BlockSpec(memory_space=pltpu.VMEM)
HBM = pl.BlockSpec(memory_space=pltpu.HBM)
SMEM = pl.BlockSpec(memory_space=pltpu.SMEM)


def shift(value, steps):
    count = lax.axis_size("blk")
    return lax.ppermute(value, "blk", [(i, (i + steps) % count) for i in range(count)])


def partner(value):
    count = lax.axis_size("blk")
    return lax.ppermute(value, "blk", [(i, i ^ 1) for i in range(count)])


def call(kernel, outs, scratch=(), specs=(), name=None, aliases=None, mib=12):
    return pl.pallas_call(
        kernel,
        out_shape=[jax.ShapeDtypeStruct(s, d) for s, d in outs],
        in_specs=list(specs),
        out_specs=[VMEM] * len(outs),
        scratch_shapes=list(scratch),
        input_output_aliases=aliases or {},
        compiler_params=pltpu.CompilerParams(vmem_limit_bytes=mib << 20),
        cost_estimate=pl.CostEstimate(flops=1000, bytes_accessed=1000, transcendentals=0),
        name=name,
    )


def column(row, rows):
    return jnp.transpose(jnp.broadcast_to(row, (LANES, rows)))


def weigh(codes, scale, points, logs, cut, weights, total):
    similarity = lax.dot_general(
        codes, points, (((1,), (1,)), ((), ())), preferred_element_type=F32
    )
    weight = jnp.exp(similarity * jnp.tile(scale, (1, TILE // LANES)) - logs[:, cut])
    weights[:, cut] = weight.astype(BF16)
    for lane in range(0, TILE, LANES):
        piece = weight[:, lane : lane + LANES]
        total = piece if total is None else total + piece
    return jnp.sum(weight, axis=0, keepdims=True), total


def row_of(total):
    return jnp.sum(jnp.transpose(total), axis=0, keepdims=True)


def tiles_of(count):
    return [slice(t * TILE, (t + 1) * TILE) for t in range(count // TILE)]


def norm_tile(raw, unit, cut):
    for start in range(cut.start, cut.stop, NORM):
        some = slice(start, start + NORM)
        wide = raw[some, :].astype(F32)
        scale = lax.rsqrt(jnp.mean(wide * wide, axis=1, keepdims=True) + 1e-06)
        unit[some, :] = (wide * scale).astype(BF16)


def block(part, codes, scales, fetch, unit, logs, weights, numer, sums, point_sum, add):
    cuts = [slice(k * part, (k + 1) * part) for k in range(codes.shape[0] // part)]
    wide = [column(scales[:, cut], part) for cut in cuts]
    totals = [None] * len(cuts)
    tiles = tiles_of(unit.shape[0])
    fetch(0)
    for t, tile in enumerate(tiles):
        points = unit[tile, :]
        if t + 1 < len(tiles):
            fetch(t + 1)
        line = 0.0
        for k, cut in enumerate(cuts):
            some, totals[k] = weigh(
                codes[cut, :], wide[k], points, logs, tile, weights.at[k], totals[k]
            )
            line = line + some
        point_sum[:, tile] = line
    for k, cut in enumerate(cuts):
        value = jnp.dot(weights[k], unit[...], preferred_element_type=F32)
        if add:
            numer[cut, :] += value
            sums[:, cut] += row_of(totals[k])
        else:
            numer[cut, :] = value
            sums[:, cut] = row_of(totals[k])


def local_kernel(
    part, odd, own_raw, other_raw, own_codes, scales, logs, other_logs,
    unit, other_unit, numer, sums, point_sum, other_sum,
    raw, codes, weights, sems, code_sem,
):
    tiles = tiles_of(unit.shape[0])

    def copies(source, at):
        return [
            pltpu.make_async_copy(source.at[tile, :], raw.at[at, tile, :], sems.at[at, t])
            for t, tile in enumerate(tiles)
        ]

    first, second = copies(own_raw, 0), copies(other_raw, 1)
    code_copy = pltpu.make_async_copy(own_codes, codes, code_sem)
    for copy in [first[0], code_copy] + first[1:] + second:
        copy.start()

    def fetch(t):
        first[t].wait()
        norm_tile(raw.at[0], unit, tiles[t])
        if t == 0:
            code_copy.wait()

    def fetch_other(t):
        second[t].wait()
        norm_tile(raw.at[1], other_unit, tiles[t])

    block(part, codes, scales, fetch, unit, logs, weights, numer, sums, point_sum, False)

    @pl.when(odd[0] == 0)
    def _():
        block(
            part, codes, scales, fetch_other, other_unit, other_logs, weights, numer, sums, other_sum, True
        )

    @pl.when(odd[0] == 1)
    def _():
        for t in range(len(tiles)):
            fetch_other(t)
        other_sum[...] = jnp.zeros_like(other_sum)


def moved_kernel(
    cut, odd, codes, scales, points, logs, others, other_logs, sums0, point_before, other_before,
    sent, sums, point_sum, other_sum, weights, numer,
):
    part, rows = cut.stop - cut.start, sums0.shape[1]
    first = scales.shape[0] - EXTRA
    scale = column(scales[first:, :rows].astype(F32)[:1, cut], part)

    def weigh_all(rows, row_logs, before, after):
        total = None
        for tile in tiles_of(rows.shape[0]):
            line, total = weigh(
                codes[:part, :], scale, rows[tile, :], row_logs, tile, weights, total
            )
            after[:, tile] = before[:, tile] + line
        return row_of(total)

    sums[...] = sums0[...]
    sums[:, cut] = weigh_all(points, logs, point_before, point_sum)

    @pl.when(odd[0] == 0)
    def _():
        other_sum[...] = other_before[...]
        value = jnp.dot(weights[...], points[...], preferred_element_type=F32)
        sent[:part, :] = value.astype(BF16)

    @pl.when(odd[0] == 1)
    def _():
        numer[...] = jnp.dot(weights[...], points[...], preferred_element_type=F32)
        sums[:, cut] += weigh_all(others, other_logs, other_before, other_sum)
        value = numer[...] + jnp.dot(weights[...], others[...], preferred_element_type=F32)
        sent[:part, :] = value.astype(BF16)


def first_rows(cut, numer, back, out):
    rows = out.shape[0]
    start = pl.multiple_of(pl.program_id(0) * rows, rows)
    total = numer[pl.ds(cut.start + start, rows), :] + back[pl.ds(start, rows), :].astype(F32)
    out[...] = total * lax.rsqrt(jnp.mean(total * total, axis=1, keepdims=True) + 1e-06)


def last_rows(cut, numer, back, sums, back_sums, before, out, mass):
    del before
    first_rows(cut, numer, back, out)
    mass[...] = jnp.log(sums[...] + back_sums[...])


def finish(cut, numer, back, *more):
    part, width = back.shape
    steps = 2
    block = part // steps
    shapes = [jax.ShapeDtypeStruct(numer.shape, F32)]
    specs = [pl.BlockSpec((block, width), lambda i: (cut.start // block + i, 0))]
    if more:
        shapes.append(jax.ShapeDtypeStruct(more[0].shape, F32))
        specs.append(VMEM)
    return pl.pallas_call(
        functools.partial(last_rows if more else first_rows, cut),
        grid=(steps,),
        out_shape=shapes,
        in_specs=[VMEM, VMEM] + ([VMEM, VMEM, HBM] if more else []),
        out_specs=specs,
        input_output_aliases={4: 0} if more else {},
        compiler_params=pltpu.CompilerParams(vmem_limit_bytes=6 << 20),
        cost_estimate=pl.CostEstimate(flops=1000, bytes_accessed=1000, transcendentals=0),
        name=f"finish{cut.start}",
    )(numer, back, *more)


def on_device(embeddings, centroid_codes, centroid_scales, log_normalizers):
    odd = (lax.axis_index("blk") & 1).astype(jnp.int32).reshape(1)
    rows, width = centroid_codes.shape
    points = embeddings.shape[0]
    half = rows // HALVES
    ends = [sum(SIZES[: k + 1]) for k in range(len(SIZES))]
    cuts = [slice(end - size, end) for end, size in zip(ends, SIZES)]
    assert ends[-1] == rows
    row = lax.broadcasted_iota(jnp.int32, (cuts[0].stop + EXTRA, rows), 0)
    first = centroid_codes[: cuts[0].stop + EXTRA]
    first = jnp.concatenate(
        [jnp.where(row < cuts[0].stop, first[:, :rows], centroid_scales), first[:, rows:]], axis=1
    )
    received = [shift(first, 2)]
    received += [shift(lax.optimization_barrier(centroid_codes)[cut], 2) for cut in cuts[1:]]
    scales = centroid_scales.astype(F32).reshape(1, rows)
    logs = log_normalizers.astype(F32).reshape(1, points)
    other_raw = partner(embeddings)
    other_logs = partner(log_normalizers).astype(F32).reshape(1, points)
    line = ((1, points), F32)
    units = ((points, width), BF16)
    unit_rows, other_rows, numer, own_sum, point_total, other_total = call(
        functools.partial(local_kernel, half),
        [units, units, ((rows, width), F32), ((1, rows), F32), line, line],
        [
            pltpu.VMEM((2, points, width), BF16),
            pltpu.VMEM((rows, width), BF16),
            pltpu.VMEM((HALVES, half, points), BF16),
            pltpu.SemaphoreType.DMA((2, points // TILE)),
            pltpu.SemaphoreType.DMA(()),
        ],
        [SMEM, HBM, HBM, HBM] + [VMEM] * 3,
        "local",
        mib=24,
    )(odd, embeddings, other_raw, centroid_codes, scales, logs, other_logs)
    back = []
    sums = jnp.zeros((1, rows), F32)
    for k, cut in enumerate(cuts):
        part = cut.stop - cut.start
        sent, sums, point_total, other_total = call(
            functools.partial(moved_kernel, cut),
            [((part, width), BF16), ((1, rows), F32), line, line],
            [pltpu.VMEM((part, points), BF16), pltpu.VMEM((part, width), F32)],
            [SMEM] + [VMEM] * 9,
            f"moved{k}",
        )(
            odd, received[k], received[0], unit_rows, logs, other_rows, other_logs, sums,
            point_total, other_total,
        )
        back.append(shift(sent, -2))
    *back[:-1], other_total, sums = lax.optimization_barrier((*back[:-1], other_total, sums))
    point_mass = jnp.log(point_total + partner(other_total))
    back_sums = shift(sums, -2)
    (new_centroids,) = finish(cuts[0], numer, back[0])
    back[1], point_mass = lax.optimization_barrier((back[1], point_mass))
    new_centroids, mass_log = finish(cuts[1], numer, back[1], own_sum, back_sums, new_centroids)
    return (new_centroids, mass_log.reshape(rows), point_mass.reshape(points))


def solution(mesh):
    return jax.shard_map(
        on_device,
        mesh=mesh,
        in_specs=(P("blk", None), P("blk", None), P("blk"), P("blk")),
        out_specs=(P("blk", None), P("blk"), P("blk")),
        check_vma=False,
    )
```

```python
import functools

import jax
import jax.numpy as jnp
from jax import lax
from jax.experimental import pallas as pl
from jax.experimental.pallas import tpu as pltpu
from jax.sharding import PartitionSpec as P

HALVES = 2
SIZES = (256, 256)
EXTRA = 16
TILE = 1024
LANES = 128
NORM = 512
F32 = jnp.float32
BF16 = jnp.bfloat16
VMEM = pl.BlockSpec(memory_space=pltpu.VMEM)
HBM = pl.BlockSpec(memory_space=pltpu.HBM)
SMEM = pl.BlockSpec(memory_space=pltpu.SMEM)


def shift(value, steps):
    count = lax.axis_size("blk")
    return lax.ppermute(value, "blk", [(i, (i + steps) % count) for i in range(count)])


def partner(value):
    count = lax.axis_size("blk")
    return lax.ppermute(value, "blk", [(i, i ^ 1) for i in range(count)])


def call(kernel, outs, scratch=(), specs=(), name=None, aliases=None, mib=12):
    return pl.pallas_call(
        kernel,
        out_shape=[jax.ShapeDtypeStruct(s, d) for s, d in outs],
        in_specs=list(specs),
        out_specs=[VMEM] * len(outs),
        scratch_shapes=list(scratch),
        input_output_aliases=aliases or {},
        compiler_params=pltpu.CompilerParams(vmem_limit_bytes=mib << 20),
        cost_estimate=pl.CostEstimate(flops=1000, bytes_accessed=1000, transcendentals=0),
        name=name,
    )


def column(row, rows):
    return jnp.transpose(jnp.broadcast_to(row, (LANES, rows)))


def weigh(codes, scale, points, logs, cut, weights, total):
    similarity = lax.dot_general(
        codes, points, (((1,), (1,)), ((), ())), preferred_element_type=F32
    )
    weight = jnp.exp(similarity * jnp.tile(scale, (1, TILE // LANES)) - logs[:, cut])
    weights[:, cut] = weight.astype(BF16)
    for lane in range(0, TILE, LANES):
        piece = weight[:, lane : lane + LANES]
        total = piece if total is None else total + piece
    return jnp.sum(weight, axis=0, keepdims=True), total


def row_of(total):
    return jnp.sum(jnp.transpose(total), axis=0, keepdims=True)


def tiles_of(count):
    return [slice(t * TILE, (t + 1) * TILE) for t in range(count // TILE)]


def norm_tile(raw, unit, cut):
    for start in range(cut.start, cut.stop, NORM):
        some = slice(start, start + NORM)
        wide = raw[some, :].astype(F32)
        scale = lax.rsqrt(jnp.mean(wide * wide, axis=1, keepdims=True) + 1e-06)
        unit[some, :] = (wide * scale).astype(BF16)


def block(part, codes, scales, fetch, unit, logs, weights, numer, sums, point_sum, add):
    cuts = [slice(k * part, (k + 1) * part) for k in range(codes.shape[0] // part)]
    wide = [column(scales[:, cut], part) for cut in cuts]
    totals = [None] * len(cuts)
    tiles = tiles_of(unit.shape[0])
    fetch(0)
    for t, tile in enumerate(tiles):
        points = unit[tile, :]
        if t + 1 < len(tiles):
            fetch(t + 1)
        line = 0.0
        for k, cut in enumerate(cuts):
            some, totals[k] = weigh(
                codes[cut, :], wide[k], points, logs, tile, weights.at[k], totals[k]
            )
            line = line + some
        point_sum[:, tile] = line
    for k, cut in enumerate(cuts):
        value = jnp.dot(weights[k], unit[...], preferred_element_type=F32)
        if add:
            numer[cut, :] += value
            sums[:, cut] += row_of(totals[k])
        else:
            numer[cut, :] = value
            sums[:, cut] = row_of(totals[k])


def local_kernel(
    part, odd, own_raw, other_raw, own_codes, scales, logs, other_logs,
    unit, other_unit, numer, sums, point_sum, other_sum,
    raw, codes, weights, sems, code_sem,
):
    tiles = tiles_of(unit.shape[0])

    def copies(source, at):
        return [
            pltpu.make_async_copy(source.at[tile, :], raw.at[at, tile, :], sems.at[at, t])
            for t, tile in enumerate(tiles)
        ]

    first, second = copies(own_raw, 0), copies(other_raw, 1)
    code_copy = pltpu.make_async_copy(own_codes, codes, code_sem)
    for copy in [first[0], code_copy] + first[1:] + second:
        copy.start()

    def fetch(t):
        first[t].wait()
        norm_tile(raw.at[0], unit, tiles[t])
        if t == 0:
            code_copy.wait()

    def fetch_other(t):
        second[t].wait()
        norm_tile(raw.at[1], other_unit, tiles[t])

    block(part, codes, scales, fetch, unit, logs, weights, numer, sums, point_sum, False)

    @pl.when(odd[0] == 0)
    def _():
        block(
            part, codes, scales, fetch_other, other_unit, other_logs, weights, numer, sums, other_sum, True
        )

    @pl.when(odd[0] == 1)
    def _():
        for t in range(len(tiles)):
            fetch_other(t)
        other_sum[...] = jnp.zeros_like(other_sum)


def moved_kernel(
    cut, odd, codes, scales, points, logs, others, other_logs, sums0, point_before, other_before,
    sent, sums, point_sum, other_sum, weights, numer,
):
    part, rows = cut.stop - cut.start, sums0.shape[1]
    first = scales.shape[0] - EXTRA
    scale = column(scales[first:, :rows].astype(F32)[:1, cut], part)

    def weigh_all(rows, row_logs, before, after):
        total = None
        for tile in tiles_of(rows.shape[0]):
            line, total = weigh(
                codes[:part, :], scale, rows[tile, :], row_logs, tile, weights, total
            )
            after[:, tile] = before[:, tile] + line
        return row_of(total)

    sums[...] = sums0[...]
    sums[:, cut] = weigh_all(points, logs, point_before, point_sum)

    @pl.when(odd[0] == 0)
    def _():
        other_sum[...] = other_before[...]
        value = jnp.dot(weights[...], points[...], preferred_element_type=F32)
        sent[:part, :] = value.astype(BF16)

    @pl.when(odd[0] == 1)
    def _():
        numer[...] = jnp.dot(weights[...], points[...], preferred_element_type=F32)
        sums[:, cut] += weigh_all(others, other_logs, other_before, other_sum)
        value = numer[...] + jnp.dot(weights[...], others[...], preferred_element_type=F32)
        sent[:part, :] = value.astype(BF16)


def first_rows(cut, numer, back, out):
    rows = out.shape[0]
    start = pl.multiple_of(pl.program_id(0) * rows, rows)
    total = numer[pl.ds(cut.start + start, rows), :] + back[pl.ds(start, rows), :].astype(F32)
    out[...] = total * lax.rsqrt(jnp.mean(total * total, axis=1, keepdims=True) + 1e-06)


def last_rows(cut, numer, back, sums, back_sums, before, out, mass):
    del before
    first_rows(cut, numer, back, out)
    mass[...] = jnp.log(sums[...] + back_sums[...])


def finish(cut, numer, back, *more):
    part, width = back.shape
    steps = 2
    block = part // steps
    shapes = [jax.ShapeDtypeStruct(numer.shape, F32)]
    specs = [pl.BlockSpec((block, width), lambda i: (cut.start // block + i, 0))]
    if more:
        shapes.append(jax.ShapeDtypeStruct(more[0].shape, F32))
        specs.append(VMEM)
    return pl.pallas_call(
        functools.partial(last_rows if more else first_rows, cut),
        grid=(steps,),
        out_shape=shapes,
        in_specs=[VMEM, VMEM] + ([VMEM, VMEM, HBM] if more else []),
        out_specs=specs,
        input_output_aliases={4: 0} if more else {},
        compiler_params=pltpu.CompilerParams(vmem_limit_bytes=6 << 20),
        cost_estimate=pl.CostEstimate(flops=1000, bytes_accessed=1000, transcendentals=0),
        name=f"finish{cut.start}",
    )(numer, back, *more)


def on_device(embeddings, centroid_codes, centroid_scales, log_normalizers):
    odd = (lax.axis_index("blk") & 1).astype(jnp.int32).reshape(1)
    rows, width = centroid_codes.shape
    points = embeddings.shape[0]
    half = rows // HALVES
    ends = [sum(SIZES[: k + 1]) for k in range(len(SIZES))]
    cuts = [slice(end - size, end) for end, size in zip(ends, SIZES)]
    assert ends[-1] == rows
    row = lax.broadcasted_iota(jnp.int32, (cuts[0].stop + EXTRA, rows), 0)
    first = centroid_codes[: cuts[0].stop + EXTRA]
    first = jnp.concatenate(
        [jnp.where(row < cuts[0].stop, first[:, :rows], centroid_scales), first[:, rows:]], axis=1
    )
    received = [shift(first, 2)]
    received += [shift(lax.optimization_barrier(centroid_codes)[cut], 2) for cut in cuts[1:]]
    scales = centroid_scales.astype(F32).reshape(1, rows)
    logs = log_normalizers.astype(F32).reshape(1, points)
    other_raw = partner(embeddings)
    other_logs = partner(log_normalizers).astype(F32).reshape(1, points)
    line = ((1, points), F32)
    units = ((points, width), BF16)
    unit_rows, other_rows, numer, own_sum, point_total, other_total = call(
        functools.partial(local_kernel, half),
        [units, units, ((rows, width), F32), ((1, rows), F32), line, line],
        [
            pltpu.VMEM((2, points, width), BF16),
            pltpu.VMEM((rows, width), BF16),
            pltpu.VMEM((HALVES, half, points), BF16),
            pltpu.SemaphoreType.DMA((2, points // TILE)),
            pltpu.SemaphoreType.DMA(()),
        ],
        [SMEM, HBM, HBM, HBM] + [VMEM] * 3,
        "local",
        mib=24,
    )(odd, embeddings, other_raw, centroid_codes, scales, logs, other_logs)
    back = []
    sums = jnp.zeros((1, rows), F32)
    for k, cut in enumerate(cuts):
        part = cut.stop - cut.start
        sent, sums, point_total, other_total = call(
            functools.partial(moved_kernel, cut),
            [((part, width), BF16), ((1, rows), F32), line, line],
            [pltpu.VMEM((part, points), BF16), pltpu.VMEM((part, width), F32)],
            [SMEM] + [VMEM] * 9,
            f"moved{k}",
        )(
            odd, received[k], received[0], unit_rows, logs, other_rows, other_logs, sums,
            point_total, other_total,
        )
        back.append(shift(sent, -2))
    *back[:-1], other_total, sums = lax.optimization_barrier((*back[:-1], other_total, sums))
    point_mass = jnp.log(point_total + partner(other_total))
    back_sums = shift(sums, -2)
    (new_centroids,) = finish(cuts[0], numer, back[0])
    back[1], point_mass = lax.optimization_barrier((back[1], point_mass))
    new_centroids, mass_log = finish(cuts[1], numer, back[1], own_sum, back_sums, new_centroids)
    return (new_centroids, mass_log.reshape(rows), point_mass.reshape(points))


def solution(mesh):
    return jax.shard_map(
        on_device,
        mesh=mesh,
        in_specs=(P("blk", None), P("blk", None), P("blk"), P("blk")),
        out_specs=(P("blk", None), P("blk"), P("blk")),
        check_vma=False,
    )
```

```python
import functools

import jax
import jax.numpy as jnp
from jax import lax
from jax.experimental import pallas as pl
from jax.experimental.pallas import tpu as pltpu
from jax.sharding import PartitionSpec as P

HALVES = 2
SIZES = (256, 256)
EXTRA = 16
TILE = 2048
LANES = 128
NORM = 256
F32 = jnp.float32
BF16 = jnp.bfloat16
VMEM = pl.BlockSpec(memory_space=pltpu.VMEM)
HBM = pl.BlockSpec(memory_space=pltpu.HBM)
SMEM = pl.BlockSpec(memory_space=pltpu.SMEM)


def shift(value, steps):
    count = lax.axis_size("blk")
    return lax.ppermute(value, "blk", [(i, (i + steps) % count) for i in range(count)])


def partner(value):
    count = lax.axis_size("blk")
    return lax.ppermute(value, "blk", [(i, i ^ 1) for i in range(count)])


def call(kernel, outs, scratch=(), specs=(), name=None, aliases=None, mib=12):
    return pl.pallas_call(
        kernel,
        out_shape=[jax.ShapeDtypeStruct(s, d) for s, d in outs],
        in_specs=list(specs),
        out_specs=[VMEM] * len(outs),
        scratch_shapes=list(scratch),
        input_output_aliases=aliases or {},
        compiler_params=pltpu.CompilerParams(vmem_limit_bytes=mib << 20),
        cost_estimate=pl.CostEstimate(flops=1000, bytes_accessed=1000, transcendentals=0),
        name=name,
    )


def column(row, rows):
    return jnp.transpose(jnp.broadcast_to(row, (LANES, rows)))


def weigh(codes, scale, points, logs, cut, weights, total):
    similarity = lax.dot_general(
        codes, points, (((1,), (1,)), ((), ())), preferred_element_type=F32
    )
    weight = jnp.exp(similarity * jnp.tile(scale, (1, TILE // LANES)) - logs[:, cut])
    weights[:, cut] = weight.astype(BF16)
    for lane in range(0, TILE, LANES):
        piece = weight[:, lane : lane + LANES]
        total = piece if total is None else total + piece
    return jnp.sum(weight, axis=0, keepdims=True), total


def row_of(total):
    return jnp.sum(jnp.transpose(total), axis=0, keepdims=True)


def tiles_of(count):
    return [slice(t * TILE, (t + 1) * TILE) for t in range(count // TILE)]


def norm_tile(raw, unit, cut):
    for start in range(cut.start, cut.stop, NORM):
        some = slice(start, start + NORM)
        wide = raw[some, :].astype(F32)
        scale = lax.rsqrt(jnp.mean(wide * wide, axis=1, keepdims=True) + 1e-06)
        unit[some, :] = (wide * scale).astype(BF16)


def block(part, codes, scales, fetch, unit, logs, weights, numer, sums, point_sum, add):
    cuts = [slice(k * part, (k + 1) * part) for k in range(codes.shape[0] // part)]
    wide = [column(scales[:, cut], part) for cut in cuts]
    totals = [None] * len(cuts)
    tiles = tiles_of(unit.shape[0])
    fetch(0)
    for t, tile in enumerate(tiles):
        points = unit[tile, :]
        if t + 1 < len(tiles):
            fetch(t + 1)
        line = 0.0
        for k, cut in enumerate(cuts):
            some, totals[k] = weigh(
                codes[cut, :], wide[k], points, logs, tile, weights.at[k], totals[k]
            )
            line = line + some
        point_sum[:, tile] = line
    for k, cut in enumerate(cuts):
        value = jnp.dot(weights[k], unit[...], preferred_element_type=F32)
        if add:
            numer[cut, :] += value
            sums[:, cut] += row_of(totals[k])
        else:
            numer[cut, :] = value
            sums[:, cut] = row_of(totals[k])


def local_kernel(
    part, odd, own_raw, other_raw, own_codes, scales, logs, other_logs,
    unit, other_unit, numer, sums, point_sum, other_sum,
    raw, codes, weights, sems, code_sem,
):
    tiles = tiles_of(unit.shape[0])

    def copies(source, at):
        return [
            pltpu.make_async_copy(source.at[tile, :], raw.at[at, tile, :], sems.at[at, t])
            for t, tile in enumerate(tiles)
        ]

    first, second = copies(own_raw, 0), copies(other_raw, 1)
    code_copy = pltpu.make_async_copy(own_codes, codes, code_sem)
    for copy in [first[0], code_copy] + first[1:] + second:
        copy.start()

    def fetch(t):
        first[t].wait()
        norm_tile(raw.at[0], unit, tiles[t])
        if t == 0:
            code_copy.wait()

    def fetch_other(t):
        second[t].wait()
        norm_tile(raw.at[1], other_unit, tiles[t])

    block(part, codes, scales, fetch, unit, logs, weights, numer, sums, point_sum, False)

    @pl.when(odd[0] == 0)
    def _():
        block(
            part, codes, scales, fetch_other, other_unit, other_logs, weights, numer, sums, other_sum, True
        )

    @pl.when(odd[0] == 1)
    def _():
        for t in range(len(tiles)):
            fetch_other(t)
        other_sum[...] = jnp.zeros_like(other_sum)


def moved_kernel(
    cut, odd, codes, scales, points, logs, others, other_logs, sums0, point_before, other_before,
    sent, sums, point_sum, other_sum, weights, numer,
):
    part, rows = cut.stop - cut.start, sums0.shape[1]
    first = scales.shape[0] - EXTRA
    scale = column(scales[first:, :rows].astype(F32)[:1, cut], part)

    def weigh_all(rows, row_logs, before, after):
        total = None
        for tile in tiles_of(rows.shape[0]):
            line, total = weigh(
                codes[:part, :], scale, rows[tile, :], row_logs, tile, weights, total
            )
            after[:, tile] = before[:, tile] + line
        return row_of(total)

    sums[...] = sums0[...]
    sums[:, cut] = weigh_all(points, logs, point_before, point_sum)

    @pl.when(odd[0] == 0)
    def _():
        other_sum[...] = other_before[...]
        value = jnp.dot(weights[...], points[...], preferred_element_type=F32)
        sent[:part, :] = value.astype(BF16)

    @pl.when(odd[0] == 1)
    def _():
        numer[...] = jnp.dot(weights[...], points[...], preferred_element_type=F32)
        sums[:, cut] += weigh_all(others, other_logs, other_before, other_sum)
        value = numer[...] + jnp.dot(weights[...], others[...], preferred_element_type=F32)
        sent[:part, :] = value.astype(BF16)


def first_rows(cut, numer, back, out):
    rows = out.shape[0]
    start = pl.multiple_of(pl.program_id(0) * rows, rows)
    total = numer[pl.ds(cut.start + start, rows), :] + back[pl.ds(start, rows), :].astype(F32)
    out[...] = total * lax.rsqrt(jnp.mean(total * total, axis=1, keepdims=True) + 1e-06)


def last_rows(cut, numer, back, sums, back_sums, before, out, mass):
    del before
    first_rows(cut, numer, back, out)
    mass[...] = jnp.log(sums[...] + back_sums[...])


def finish(cut, numer, back, *more):
    part, width = back.shape
    steps = 2
    block = part // steps
    shapes = [jax.ShapeDtypeStruct(numer.shape, F32)]
    specs = [pl.BlockSpec((block, width), lambda i: (cut.start // block + i, 0))]
    if more:
        shapes.append(jax.ShapeDtypeStruct(more[0].shape, F32))
        specs.append(VMEM)
    return pl.pallas_call(
        functools.partial(last_rows if more else first_rows, cut),
        grid=(steps,),
        out_shape=shapes,
        in_specs=[VMEM, VMEM] + ([VMEM, VMEM, HBM] if more else []),
        out_specs=specs,
        input_output_aliases={4: 0} if more else {},
        compiler_params=pltpu.CompilerParams(vmem_limit_bytes=6 << 20),
        cost_estimate=pl.CostEstimate(flops=1000, bytes_accessed=1000, transcendentals=0),
        name=f"finish{cut.start}",
    )(numer, back, *more)


def on_device(embeddings, centroid_codes, centroid_scales, log_normalizers):
    odd = (lax.axis_index("blk") & 1).astype(jnp.int32).reshape(1)
    rows, width = centroid_codes.shape
    points = embeddings.shape[0]
    half = rows // HALVES
    ends = [sum(SIZES[: k + 1]) for k in range(len(SIZES))]
    cuts = [slice(end - size, end) for end, size in zip(ends, SIZES)]
    assert ends[-1] == rows
    row = lax.broadcasted_iota(jnp.int32, (cuts[0].stop + EXTRA, rows), 0)
    first = centroid_codes[: cuts[0].stop + EXTRA]
    first = jnp.concatenate(
        [jnp.where(row < cuts[0].stop, first[:, :rows], centroid_scales), first[:, rows:]], axis=1
    )
    received = [shift(first, 2)]
    received += [shift(lax.optimization_barrier(centroid_codes)[cut], 2) for cut in cuts[1:]]
    scales = centroid_scales.astype(F32).reshape(1, rows)
    logs = log_normalizers.astype(F32).reshape(1, points)
    other_raw = partner(embeddings)
    other_logs = partner(log_normalizers).astype(F32).reshape(1, points)
    line = ((1, points), F32)
    units = ((points, width), BF16)
    unit_rows, other_rows, numer, own_sum, point_total, other_total = call(
        functools.partial(local_kernel, half),
        [units, units, ((rows, width), F32), ((1, rows), F32), line, line],
        [
            pltpu.VMEM((2, points, width), BF16),
            pltpu.VMEM((rows, width), BF16),
            pltpu.VMEM((HALVES, half, points), BF16),
            pltpu.SemaphoreType.DMA((2, points // TILE)),
            pltpu.SemaphoreType.DMA(()),
        ],
        [SMEM, HBM, HBM, HBM] + [VMEM] * 3,
        "local",
        mib=24,
    )(odd, embeddings, other_raw, centroid_codes, scales, logs, other_logs)
    back = []
    sums = jnp.zeros((1, rows), F32)
    for k, cut in enumerate(cuts):
        part = cut.stop - cut.start
        sent, sums, point_total, other_total = call(
            functools.partial(moved_kernel, cut),
            [((part, width), BF16), ((1, rows), F32), line, line],
            [pltpu.VMEM((part, points), BF16), pltpu.VMEM((part, width), F32)],
            [SMEM] + [VMEM] * 9,
            f"moved{k}",
        )(
            odd, received[k], received[0], unit_rows, logs, other_rows, other_logs, sums,
            point_total, other_total,
        )
        back.append(shift(sent, -2))
    *back[:-1], other_total, sums = lax.optimization_barrier((*back[:-1], other_total, sums))
    point_mass = jnp.log(point_total + partner(other_total))
    back_sums = shift(sums, -2)
    (new_centroids,) = finish(cuts[0], numer, back[0])
    back[1], point_mass = lax.optimization_barrier((back[1], point_mass))
    new_centroids, mass_log = finish(cuts[1], numer, back[1], own_sum, back_sums, new_centroids)
    return (new_centroids, mass_log.reshape(rows), point_mass.reshape(points))


def solution(mesh):
    return jax.shard_map(
        on_device,
        mesh=mesh,
        in_specs=(P("blk", None), P("blk", None), P("blk"), P("blk")),
        out_specs=(P("blk", None), P("blk"), P("blk")),
        check_vma=False,
    )
```
